256 devices in a mesh: seq: 16 (over y, x), row: 2 (over core), col: 8 (over z).
Axes of the slice: x: 4, y: 4, z: 8, core: 2. Of those that a mesh axis runs over, the one named last changes fastest.
Arguments:
- projected: bfloat16 [3, 16, 1024, 4096], P(None, 'col', 'seq', 'row'), may hold values from -160 to 160
- out_weight: bfloat16 [4096, 6144], P('row', 'col'), may hold values from -0.75 to 0.75
- cotangent: bfloat16 [16, 1024, 6144], P('row', 'seq', 'col'), may hold values from -0.59765625 to 0.59765625
Outputs:
- mixed_tokens: bfloat16 [16, 1024, 6144], P('row', 'seq', 'col')
- weight_grad: float32 [4096, 6144], P('row', 'col')
The draws below stay inside these ranges and needn't reach their ends.
All inputs are finite; a program needn't handle non-finite values.
Results may differ from the reference program's by a relative error of at most 0.018.
Values may be sent and summed in bfloat16 or wider, within the bound.
No kernel may reach another device: no remote copies, remote signals or barrier semaphores. Data moves between devices by JAX's collectives and lax.ppermute only.
A program may use at most 128 MiB of HBM per device.

```python
import math
import jax
import jax.numpy as jnp
from jax import lax

D = 6144
HEADS = 32
HEAD_DIM = 128
LENGTH = 1024
INNER = 4096
BATCH = 16


def draw_projected(key, part):
    key = jax.random.fold_in(key, 11)
    subkeys = jax.random.split(key, 1)
    normals = jnp.clip(jax.random.normal(subkeys[0], (3, BATCH, LENGTH, INNER), jnp.float32), -5.0, 5.0)
    queries = 1.5 * normals[0]
    key_rows = normals[1]
    value_rows = normals[2]
    return jnp.stack([queries, key_rows, value_rows]).astype(jnp.bfloat16)


def shard_levels(own_key, shape, cuts, smallest, top_value):
    gain = 1.0
    for axis_at, parts in cuts:
        steps = jax.random.uniform(jax.random.fold_in(jax.random.fold_in(own_key, 6), axis_at), (parts,), jnp.float32, smallest / len(cuts), top_value / len(cuts))
        gain = gain * jnp.repeat(jnp.exp(steps), shape[axis_at] // parts).reshape((-1,) + (1,) * (len(shape) - 1 - axis_at))
    return gain


def bell_draw(rng, shape, deviation, reach, cuts=(), held_as=jnp.bfloat16):
    result = jax.random.normal(rng, shape, jnp.float32) * deviation
    if len(cuts) > 0:
        result = shard_levels(rng, shape, cuts, -0.22, 0.18) * result
    return jnp.clip(result, min=-reach, max=reach).astype(held_as)


def setup_inputs(seed: int = 0) -> dict:
    seeds = jax.random.split(jax.random.key(seed), 4)
    projected = draw_projected(jax.random.fold_in(seeds[3], 71), 0)
    out_weight = bell_draw(seeds[1], (INNER, D), (INNER // 64) ** -0.5, 0.75, ((0, 2), (1, 8)))
    cotangent = bell_draw(seeds[2], (BATCH, LENGTH, D), 0.1, 0.59765625, ((0, 2), (1, 16), (2, 8)))
    return {"projected": projected, "out_weight": out_weight, "cotangent": cotangent}


def one_head(operands):
    head_query, head_key, head_value = operands
    scores = jnp.dot(head_query, head_key.T, preferred_element_type=jnp.float32) * (1.0 / math.sqrt(HEAD_DIM))
    row_max = lax.optimization_barrier(jnp.max(scores, axis=1, keepdims=True))
    exp_scores = jnp.exp(scores - row_max)
    numerator = jnp.dot(exp_scores.astype(jnp.bfloat16), head_value, preferred_element_type=jnp.float32)
    return (numerator / lax.optimization_barrier(jnp.sum(exp_scores, axis=1, keepdims=True))).astype(jnp.bfloat16)

def reference(projected, out_weight, cotangent):
    heads_first = projected.reshape(3, BATCH, LENGTH, HEADS, HEAD_DIM).transpose(0, 1, 3, 2, 4)
    heads_first = heads_first.reshape(3, BATCH * HEADS, LENGTH, HEAD_DIM)
    attended = lax.map(one_head, (heads_first[0], heads_first[1], heads_first[2]))
    attended = attended.reshape(BATCH, HEADS, LENGTH, HEAD_DIM).transpose(0, 2, 1, 3).reshape(BATCH * LENGTH, INNER)
    mixed_tokens = jnp.dot(attended, out_weight, preferred_element_type=jnp.float32).astype(jnp.bfloat16)
    mixed_tokens = mixed_tokens.reshape(BATCH, LENGTH, D)
    weight_grad = jnp.dot(attended.T, cotangent.reshape(BATCH * LENGTH, D), preferred_element_type=jnp.float32)
    return (mixed_tokens, weight_grad)
```

```python
import math

import jax
import jax.numpy as jnp
from jax import lax
from jax.experimental import pallas as pl
from jax.experimental.pallas import tpu as pltpu
from jax.sharding import Mesh, PartitionSpec as P

HEAD_DIM = 128
F32 = jnp.float32
BF16 = jnp.bfloat16
Y = ("yh", "yl")
SEQ = ("yh", "yl", "x")
MIB = 1024 * 1024


def ring(size, shift):
    return [(i, (i + shift) % size) for i in range(size)]


def tied(*values):
    return lax.optimization_barrier(values)


def shift_z(value, step):
    return lax.ppermute(value, "col", ring(8, step))


def shift_plane(value, axis, step):
    return lax.ppermute(value, axis, ring(4, step))


def attention_kernel(place, parts, keep, send, by_block):
    core = place[0]
    scale = math.log2(math.e) / math.sqrt(HEAD_DIM)
    for b in range(2):
        keys = parts[:, 1, b].reshape(1024, HEAD_DIM)
        values = parts[:, 2, b].reshape(1024, HEAD_DIM)
        for far in range(2):
            rows = pl.ds(pl.multiple_of(32 * lax.rem(core + far, 2), 32), 32)
            target = send if far else keep
            for j in range(2):
                queries = parts[8 * j : 8 * j + 8, 0, b, rows].reshape(256, HEAD_DIM)
                scores = lax.dot_general(
                    queries, keys, (((1,), (1,)), ((), ())), preferred_element_type=F32
                )
                top = jnp.max(scores, axis=1, keepdims=True)
                exps = jnp.exp2((scores - top) * scale)
                total = jnp.sum(exps, axis=1, keepdims=True)
                out = jnp.dot(exps.astype(BF16), values, preferred_element_type=F32) / total
                target[b, :, 256 * j : 256 * j + 256] = out.T.astype(BF16)
                by_block[8 * j : 8 * j + 8, b, rows] = out.astype(BF16).reshape(8, 32, HEAD_DIM)


def attention(parts, core):
    return pl.pallas_call(
        attention_kernel,
        out_shape=(
            jax.ShapeDtypeStruct((2, HEAD_DIM, 512), BF16),
            jax.ShapeDtypeStruct((2, HEAD_DIM, 512), BF16),
            jax.ShapeDtypeStruct((16, 2, 64, HEAD_DIM), BF16),
        ),
        in_specs=[
            pl.BlockSpec(memory_space=pltpu.SMEM),
            pl.BlockSpec(memory_space=pltpu.VMEM),
        ],
        out_specs=[pl.BlockSpec(memory_space=pltpu.VMEM)] * 3,
        compiler_params=pltpu.CompilerParams(vmem_limit_bytes=40 * MIB),
        cost_estimate=pl.CostEstimate(
            flops=1100000000, bytes_accessed=3 * MIB, transcendentals=2 * MIB
        ),
        name="attention",
    )(core, parts)


def grad_kernel(place, cotangents, *refs):
    blocks, (out, held, sems) = refs[:-3], refs[-3:]
    count = len(blocks) // 2

    def copy(j):
        source = cotangents.at[:, pl.ds(place[j], 2)]
        return pltpu.make_async_copy(source, held.at[j % 2], sems.at[j % 2])

    copy(0).start()
    for j in range(count):
        if j + 1 < count:
            copy(j + 1).start()
        copy(j).wait()
        total = None
        for b in range(2):
            rows = jnp.concatenate([blocks[2 * j][b], blocks[2 * j + 1][b]], axis=0)
            right = held[j % 2, :, b].reshape(512, 768)
            term = jnp.dot(rows, right, preferred_element_type=F32)
            total = term if total is None else total + term
        if j == 0:
            out[...] = total
        else:
            out[...] += total


def weight_grad_rows(place, cotangents, blocks):
    return pl.pallas_call(
        grad_kernel,
        out_shape=jax.ShapeDtypeStruct((256, 768), F32),
        in_specs=[
            pl.BlockSpec(memory_space=pltpu.SMEM),
            pl.BlockSpec(memory_space=pl.ANY),
        ]
        + [pl.BlockSpec(memory_space=pltpu.VMEM)] * len(blocks),
        out_specs=pl.BlockSpec(memory_space=pltpu.VMEM),
        scratch_shapes=[
            pltpu.VMEM((2, 16, 2, 32, 768), BF16),
            pltpu.SemaphoreType.DMA((2,)),
        ],
        compiler_params=pltpu.CompilerParams(vmem_limit_bytes=40 * MIB),
        cost_estimate=pl.CostEstimate(
            flops=3200000000, bytes_accessed=17 * MIB, transcendentals=0
        ),
        name="weight_grad_rows",
    )(place, cotangents, *blocks)


def assemble_kernel(place, *refs):
    out = refs[-1]
    y, x = place[0], place[1]
    dy = lax.rem(y - pl.program_id(0) + 4, 4)
    for column in range(4):
        dx = lax.rem(x - column + 4, 4)
        for half in range(2):
            pieces = refs[8 * half : 8 * half + 8]
            ringed, direct = (dy, dx) if half == 0 else (dx, dy)
            for slot, distance in enumerate((0, 1, 3, 2)):
                for pair in range(2):

                    @pl.when((ringed == distance) & (direct // 2 == pair))
                    def _():
                        piece = pieces[2 * slot + pair][lax.rem(direct, 2)]
                        out[column, half] = piece.astype(F32)


def assemble(place, pieces):
    return pl.pallas_call(
        assemble_kernel,
        grid=(4,),
        out_shape=jax.ShapeDtypeStruct((16, 2, 64, 768), F32),
        in_specs=[pl.BlockSpec(memory_space=pltpu.SMEM)]
        + [pl.BlockSpec(memory_space=pltpu.VMEM)] * len(pieces),
        out_specs=pl.BlockSpec((4, 2, 64, 768), lambda i: (i, 0, 0, 0)),
        compiler_params=pltpu.CompilerParams(vmem_limit_bytes=32 * MIB),
        cost_estimate=pl.CostEstimate(
            flops=2 * MIB, bytes_accessed=9 * MIB, transcendentals=0
        ),
        name="assemble",
    )(place, *pieces)


def by_distance(value, axis):
    one, two, three = (shift_plane(value, axis, d) for d in (1, 2, 3))
    return jnp.stack([value, one]), jnp.stack([two, three])


def around(pairs, axis):
    first, second = pairs
    back = shift_plane(first, axis, 1), shift_plane(second, axis, 1)
    ahead = shift_plane(first, axis, -1), shift_plane(second, axis, -1)
    far = shift_plane(back[0], axis, 1), shift_plane(ahead[1], axis, -1)
    return [first, second, *back, *ahead, *far]


def swap_cores(value):
    return lax.ppermute(value, "row", [(0, 1), (1, 0)])


def per_device(projected, out_weight, cotangent):
    yh, yl, x = (lax.axis_index(a) for a in SEQ)
    y = 2 * yh + yl
    core, z = lax.axis_index("row"), lax.axis_index("col")

    given = swap_cores(lax.dynamic_slice_in_dim(cotangent, 32 * (1 - core), 32, 1))
    own = lax.dynamic_slice_in_dim(cotangent, 32 * core, 32, 1)
    cotangents = lax.all_gather(jnp.concatenate([own, given]), SEQ, axis=0)

    by_head = projected.reshape(3, 2, 64, 16, HEAD_DIM).transpose(3, 0, 1, 2, 4)
    parts = lax.all_to_all(by_head, SEQ, 0, 0, tiled=True)
    keep, send, by_block = attention(parts, core.reshape(1))

    other = swap_cores(send)
    blocks, order = [keep, other], [z]
    k_up = k_down = keep
    o_up = o_down = other
    for d in (1, 2, 3):
        if d == 2:
            k_up, k_down, o_up, o_down = tied(k_up, k_down, o_up, o_down)
            heads = lax.all_to_all(by_block, SEQ, 0, 0, tiled=True)
            tokens = heads.transpose(1, 2, 0, 3).reshape(128, 2048)
        if d == 3:
            k_up, k_down, o_up, o_down, tokens = tied(k_up, k_down, o_up, o_down, tokens)
        k_up, k_down = shift_z(k_up, 1), shift_z(k_down, -1)
        o_up, o_down = shift_z(o_up, 1), shift_z(o_down, -1)
        blocks += [k_up, o_up, k_down, o_down]
        order += [(z - d) % 8, (z + d) % 8]
    k_up, k_down, o_up, o_down = tied(k_up, k_down, o_up, o_down)
    blocks += [shift_z(k_up, 1), shift_z(o_down, -1)]
    order += [(z + 4) % 8]
    gathered = lax.all_gather(tokens, "col", axis=0, tiled=True)
    order = (2 * jnp.stack(order) + 8 * core) % 16
    partial = weight_grad_rows(order, cotangents, blocks)
    got = swap_cores(partial[128:].astype(BF16))
    rows = (partial[:128] + got.astype(F32)).astype(BF16)
    top, bottom = by_distance(rows[:64], "x"), by_distance(rows[64:], Y)
    top, bottom = around(top, Y), around(bottom, "x")
    gathered, top[6], top[7], bottom[6], bottom[7] = tied(
        gathered, top[6], top[7], bottom[6], bottom[7]
    )
    weight_grad = assemble(jnp.stack([y, x]), top + bottom).reshape(2048, 768)

    def project(which):
        part = lax.dynamic_slice_in_dim(gathered, which * 512, 512)
        return jnp.dot(part, out_weight, preferred_element_type=F32)

    sent = swap_cores(project(1 - core).astype(BF16))
    mixed = (project(core) + sent.astype(F32)).astype(BF16).reshape(8, 64, 768)
    return mixed, weight_grad


def solution(mesh):
    fine = Mesh(mesh.devices.reshape(2, 2, 4, 2, 8), SEQ + ("row", "col"))
    return jax.shard_map(
        per_device,
        mesh=fine,
        in_specs=(P(None, "col", SEQ, "row"), P("row", "col"), P("row", SEQ, "col")),
        out_specs=(P("row", SEQ, "col"), P("row", "col")),
        check_vma=False,
    )
```

```python
import math

import jax
import jax.numpy as jnp
from jax import lax
from jax.experimental import pallas as pl
from jax.experimental.pallas import tpu as pltpu
from jax.sharding import Mesh, PartitionSpec as P

HEAD_DIM = 128
F32 = jnp.float32
BF16 = jnp.bfloat16
Y = ("yh", "yl")
SEQ = ("yh", "yl", "x")
MIB = 1024 * 1024


def ring(size, shift):
    return [(i, (i + shift) % size) for i in range(size)]


def tied(*values):
    return lax.optimization_barrier(values)


def pairwise_tied(one, two):
    values = tied(*one, *two)
    return tuple(values[:2]), tuple(values[2:])


def shift_z(value, step):
    return lax.ppermute(value, "col", ring(8, step))


def shift_plane(value, axis, step):
    return lax.ppermute(value, axis, ring(4, step))


def attention_kernel(place, parts, keep, chip, by_block):
    core, upper, lower = place[0], place[1], place[2]
    scale = math.log2(math.e) / math.sqrt(HEAD_DIM)
    for b in range(2):
        keys = parts[:, 1, b].reshape(1024, HEAD_DIM)
        values = parts[:, 2, b].reshape(1024, HEAD_DIM)
        for far in range(2):
            rows = pl.ds(pl.multiple_of(32 * lax.rem(core + far, 2), 32), 32)
            target = chip if far else keep
            for away in range(2):
                span = pl.ds(8 * lax.rem(upper + away, 2), 8)
                queries = parts[span, 0, b, rows].reshape(256, HEAD_DIM)
                scores = lax.dot_general(
                    queries, keys, (((1,), (1,)), ((), ())), preferred_element_type=F32
                )
                top = jnp.max(scores, axis=1, keepdims=True)
                exps = jnp.exp2((scores - top) * scale)
                total = jnp.sum(exps, axis=1, keepdims=True)
                out = jnp.dot(exps.astype(BF16), values, preferred_element_type=F32) / total
                turned = out.T.astype(BF16)
                for low in range(2):
                    row = 2 * away + lax.rem(lower + low, 2)
                    columns = slice(128 * b, 128 * b + 128)
                    target[row, :, columns] = turned[:, 128 * low : 128 * low + 128]
                by_block[span, b, rows] = out.astype(BF16).reshape(8, 32, HEAD_DIM)


def attention(place, parts):
    quarters = jax.ShapeDtypeStruct((4, HEAD_DIM, 256), BF16)
    return pl.pallas_call(
        attention_kernel,
        out_shape=(quarters, quarters, jax.ShapeDtypeStruct((16, 2, 64, HEAD_DIM), BF16)),
        in_specs=[
            pl.BlockSpec(memory_space=pltpu.SMEM),
            pl.BlockSpec(memory_space=pltpu.VMEM),
        ],
        out_specs=[pl.BlockSpec(memory_space=pltpu.VMEM)] * 3,
        compiler_params=pltpu.CompilerParams(vmem_limit_bytes=58 * MIB),
        cost_estimate=pl.CostEstimate(
            flops=1100000000, bytes_accessed=3 * MIB, transcendentals=2 * MIB
        ),
        name="attention",
    )(place, parts)


def add_blocks(place, cotangents, blocks, held, taken, sems, total, before=None):
    count = len(blocks) // 2
    x = place[count]

    def copies(j):
        for distance, source in enumerate(cotangents):
            yield pltpu.make_async_copy(
                source.at[pl.ds(place[j], 2)],
                held.at[j % 2, :, lax.rem(x - distance + 4, 4)],
                sems.at[j % 2, distance],
            )
        for half in range(2):
            yield pltpu.make_async_copy(
                blocks[2 * j + half],
                taken.at[j % 2, 4 * half : 4 * half + 4],
                sems.at[j % 2, 4 + half],
            )

    def start(j):
        for copy in copies(j):
            copy.start()

    start(0)
    for j in range(count):
        if j + 1 < count:
            start(j + 1)
        for copy in copies(j):
            copy.wait()
        left, right = taken[j % 2].reshape(1024, 256), held[j % 2].reshape(256, 768)
        term = jnp.dot(left, right, preferred_element_type=F32)
        if j > 0:
            total[...] += term
        elif before is None:
            total[...] = term
        else:
            total[...] = before[...] + term


def early_kernel(place, *refs):
    blocks, (out, held, taken, sems) = refs[4:-4], refs[-4:]
    add_blocks(place, refs[:4], blocks, held, taken, sems, out)


def late_kernel(place, *refs):
    blocks, (sent, kept, held, taken, sems, total) = refs[5:-6], refs[-6:]
    add_blocks(place, refs[:4], blocks, held, taken, sems, total, refs[4])
    for i in range(4):
        kept[i] = total[256 * i : 256 * i + 128]
        sent[i] = total[256 * i + 128 : 256 * i + 256].astype(BF16)


def grad_call(kernel, name, out_shape, place, cotangents, before, blocks, extra):
    vmem = pl.BlockSpec(memory_space=pltpu.VMEM)
    anywhere = pl.BlockSpec(memory_space=pl.ANY)
    count = len(blocks) // 2
    return pl.pallas_call(
        kernel,
        out_shape=out_shape,
        in_specs=[pl.BlockSpec(memory_space=pltpu.SMEM)]
        + [anywhere] * 4
        + [vmem] * len(before)
        + [anywhere] * len(blocks),
        out_specs=jax.tree.map(lambda _: vmem, out_shape),
        scratch_shapes=[
            pltpu.VMEM((2, 2, 4, 32, 768), BF16),
            pltpu.VMEM((2, 8, 128, 256), BF16),
            pltpu.SemaphoreType.DMA((2, 6)),
        ]
        + extra,
        compiler_params=pltpu.CompilerParams(vmem_limit_bytes=58 * MIB),
        cost_estimate=pl.CostEstimate(
            flops=400000000 * count, bytes_accessed=2 * MIB * count, transcendentals=0
        ),
        name=name,
    )(place, *cotangents, *before, *blocks)


def project_kernel(place, *refs):
    nears, fars, weight = refs[:4], refs[4:9], refs[9]
    others, mine, left, sems = refs[10:]

    def copies(d, swapped):
        at = 128 * place[4 + d]
        yield pltpu.make_async_copy(
            nears[d], left.at[swapped, pl.ds(pl.multiple_of(at, 128), 128)], sems.at[d, 0]
        )
        for half, source in enumerate(fars[:2] if d == 0 else fars[d + 1 : d + 2]):
            size = source.shape[0]
            rows = pl.ds(pl.multiple_of(at + size * half, size), size)
            yield pltpu.make_async_copy(source, left.at[1 - swapped, rows], sems.at[d, 1 + half])

    for d in range(4):
        for copy in copies(d, place[d]):
            copy.start()
    for d in range(4):
        for copy in copies(d, place[d]):
            copy.wait()
    for which, out in ((0, others), (1, mine)):
        product = jnp.dot(left[which], weight[...], preferred_element_type=F32)
        out[...] = product.astype(out.dtype)


def project(place, nears, fars, weight):
    vmem = pl.BlockSpec(memory_space=pltpu.VMEM)
    return pl.pallas_call(
        project_kernel,
        out_shape=(
            jax.ShapeDtypeStruct((512, 768), BF16),
            jax.ShapeDtypeStruct((512, 768), F32),
        ),
        in_specs=[pl.BlockSpec(memory_space=pltpu.SMEM)]
        + [pl.BlockSpec(memory_space=pl.ANY)] * 9
        + [vmem],
        out_specs=(vmem, vmem),
        scratch_shapes=[pltpu.VMEM((2, 512, 2048), BF16), pltpu.SemaphoreType.DMA((4, 3))],
        compiler_params=pltpu.CompilerParams(vmem_limit_bytes=58 * MIB),
        cost_estimate=pl.CostEstimate(
            flops=3200000000, bytes_accessed=10 * MIB, transcendentals=0
        ),
        name="project",
    )(place, *nears, *fars, weight)


def assemble_kernel(place, *refs):
    out = refs[-1]
    y, x = place[0], place[1]
    dy = lax.rem(y - pl.program_id(0) + 4, 4)
    for column in range(4):
        dx = lax.rem(x - column + 4, 4)
        for half in range(2):
            ringed, direct = (dy, dx) if half == 0 else (dx, dy)
            for distance in range(4):

                @pl.when(ringed == distance)
                def _():
                    out[column, half] = refs[4 * half + distance][direct].astype(F32)


def assemble(place, pieces):
    return pl.pallas_call(
        assemble_kernel,
        grid=(4,),
        out_shape=jax.ShapeDtypeStruct((16, 2, 64, 768), F32),
        in_specs=[pl.BlockSpec(memory_space=pltpu.SMEM)]
        + [pl.BlockSpec(memory_space=pltpu.VMEM)] * len(pieces),
        out_specs=pl.BlockSpec((4, 2, 64, 768), lambda i: (i, 0, 0, 0)),
        compiler_params=pltpu.CompilerParams(vmem_limit_bytes=58 * MIB),
        cost_estimate=pl.CostEstimate(
            flops=2 * MIB, bytes_accessed=9 * MIB, transcendentals=0
        ),
        name="assemble",
    )(place, *pieces)


def by_distance(value, axis):
    return jnp.stack([value] + [shift_plane(value, axis, d) for d in (1, 2, 3)])


def around(value, axis, way):
    back, ahead = shift_plane(value, axis, 1), shift_plane(value, axis, -1)
    return [value, back, shift_plane(back if way > 0 else ahead, axis, way), ahead]


def swap_cores(value):
    return lax.ppermute(value, "row", [(0, 1), (1, 0)])


def swap_rows(value, mask):
    return lax.ppermute(value, Y, [(i, i ^ mask) for i in range(4)])


def per_device(projected, out_weight, cotangent):
    yh, yl, x = (lax.axis_index(a) for a in SEQ)
    y = 2 * yh + yl
    core, z = lax.axis_index("row"), lax.axis_index("col")

    by_head = projected.reshape(3, 2, 64, 16, HEAD_DIM).transpose(3, 0, 1, 2, 4)
    parts = lax.all_to_all(by_head, SEQ, 0, 0, tiled=True)

    given = swap_cores(lax.dynamic_slice_in_dim(cotangent, 32 * (1 - core), 32, 1))
    own = lax.dynamic_slice_in_dim(cotangent, 32 * core, 32, 1)
    own = jnp.concatenate([own, given])
    back, ahead = shift_plane(own, "x", 1), shift_plane(own, "x", -1)

    keep, chip, by_block = attention(jnp.stack([core, yh, yl]), parts)
    chip = swap_cores(chip)
    mine, *others = (jnp.stack([keep[e], chip[e]]) for e in range(4))
    heads = [mine] + [swap_rows(v, e + 1) for e, v in enumerate(others)]
    block, other = jnp.concatenate(heads[:2]), jnp.concatenate(heads[2:])

    first, second, order = [(block, block)], [(other, other)], [z]
    for d in (1, 2, 3):
        if d > 1:
            *first[-1:], second[-2] = pairwise_tied(first[-1], second[-2])
        first.append((shift_z(first[-1][0], 1), shift_z(first[-1][1], -1)))
        second.append((shift_z(second[-1][0], 1), shift_z(second[-1][1], -1)))
        order += [(z - d) % 8, (z + d) % 8]
        if d == 1:
            ahead, *first[1:], by_block, back = tied(ahead, first[1], by_block, back)
            low, high = shift_plane(back[:8], "x", 1), shift_plane(ahead[8:], "x", -1)
            cotangents = [own, back, jnp.concatenate([low, high]), ahead]
            heads = lax.all_to_all(by_block, SEQ, 0, 0, tiled=True)
            tokens = heads.transpose(1, 2, 0, 3).reshape(128, 2048)
    first[3], second[3] = pairwise_tied(first[3], second[3])
    last = shift_z(first[3][0], 1), shift_z(second[3][1], -1)
    *last, tokens = tied(*last, tokens)
    blocks = [first[0][0], second[0][0]]
    for one, two in zip(first[1:], second[1:]):
        blocks += [one[0], two[0], one[1], two[1]]
    blocks += last
    order = (2 * jnp.stack(order + [(z + 4) % 8]) + 8 * core) % 16
    spot = x.reshape(1)
    rows = jax.ShapeDtypeStruct((1024, 768), F32)
    early = grad_call(
        early_kernel,
        "early",
        rows,
        jnp.concatenate([order[:5], spot]),
        cotangents,
        [],
        blocks[:10],
        [],
    )
    sent, kept = grad_call(
        late_kernel,
        "late",
        (
            jax.ShapeDtypeStruct((4, 128, 768), BF16),
            jax.ShapeDtypeStruct((4, 128, 768), F32),
        ),
        jnp.concatenate([order[5:], spot]),
        cotangents,
        [early],
        blocks[10:],
        [pltpu.VMEM((1024, 768), F32)],
    )
    kept = kept + swap_cores(sent).astype(F32)
    rows = kept[0]
    for e in (1, 2, 3):
        rows = rows + swap_rows(kept[e].astype(BF16), e).astype(F32)
    rows = rows.astype(BF16)

    ups, downs = [tokens, shift_z(tokens, 1)], [tokens, shift_z(tokens, -1)]
    ups[1], downs[1], rows = tied(ups[1], downs[1], rows)
    ups.append(shift_z(ups[1], 1))
    downs.append(shift_z(downs[1], -1))
    top, bottom = by_distance(rows[:64], "x"), by_distance(rows[64:], Y)
    ups[2], downs[2], top, bottom = tied(ups[2], downs[2], top, bottom)
    ups.append(shift_z(ups[2], 1))
    downs.append(shift_z(downs[2], -1))
    top, bottom = around(top, Y, 1), around(bottom, "x", -1)
    ups[3], downs[3], top[1], top[3], bottom[1], bottom[3] = tied(
        ups[3], downs[3], top[1], top[3], bottom[1], bottom[3]
    )
    last = [shift_z(ups[3][:64], 1), shift_z(downs[3][64:], -1)]
    *last, top[2], bottom[2] = tied(*last, top[2], bottom[2])
    here = [((z - d) % 8 // 4 == core).astype(jnp.int32) for d in range(4)]
    slots = [(z - d) % 4 for d in range(4)]
    sent, mine = project(
        jnp.stack(here + slots), ups, last + [downs[3], downs[2], downs[1]], out_weight
    )
    sent = swap_cores(sent)
    mine, top[2], bottom[2] = tied(mine, top[2], bottom[2])
    weight_grad = assemble(jnp.stack([y, x]), top + bottom).reshape(2048, 768)
    mixed = (mine + sent.astype(F32)).astype(BF16).reshape(8, 64, 768)
    return mixed, weight_grad


def solution(mesh):
    fine = Mesh(mesh.devices.reshape(2, 2, 4, 2, 8), SEQ + ("row", "col"))
    return jax.shard_map(
        per_device,
        mesh=fine,
        in_specs=(P(None, "col", SEQ, "row"), P("row", "col"), P("row", SEQ, "col")),
        out_specs=(P("row", SEQ, "col"), P("row", "col")),
        check_vma=False,
    )
```

```python
import functools
import math

import jax
import jax.numpy as jnp
from jax import lax
from jax.experimental import pallas as pl
from jax.experimental.pallas import tpu as pltpu
from jax.sharding import Mesh, PartitionSpec as P

HEAD_DIM = 128
F32 = jnp.float32
BF16 = jnp.bfloat16
Y = ("yh", "yl")
SEQ = ("yh", "yl", "x")
MIB = 1024 * 1024


def ring(size, shift):
    return [(i, (i + shift) % size) for i in range(size)]


def tied(*values):
    return lax.optimization_barrier(values)


def pairwise_tied(one, two):
    values = tied(*one, *two)
    return tuple(values[:2]), tuple(values[2:])


def shift_z(value, step):
    return lax.ppermute(value, "col", ring(8, step))


def shift_plane(value, axis, step):
    return lax.ppermute(value, axis, ring(4, step))


def attention_kernel(place, parts, keep, chip, by_block):
    core, upper, lower = place[0], place[1], place[2]
    scale = math.log2(math.e) / math.sqrt(HEAD_DIM)
    for b in range(2):
        keys = parts[:, 1, b].reshape(1024, HEAD_DIM)
        values = parts[:, 2, b].reshape(1024, HEAD_DIM)
        for far in range(2):
            rows = pl.ds(pl.multiple_of(32 * lax.rem(core + far, 2), 32), 32)
            target = chip if far else keep
            for away in range(2):
                span = pl.ds(8 * lax.rem(upper + away, 2), 8)
                queries = parts[span, 0, b, rows].reshape(256, HEAD_DIM)
                scores = lax.dot_general(
                    queries, keys, (((1,), (1,)), ((), ())), preferred_element_type=F32
                )
                top = jnp.max(scores, axis=1, keepdims=True)
                exps = jnp.exp2((scores - top) * scale)
                total = jnp.sum(exps, axis=1, keepdims=True)
                out = jnp.dot(exps.astype(BF16), values, preferred_element_type=F32) / total
                turned = out.T.astype(BF16)
                for low in range(2):
                    row = 2 * away + lax.rem(lower + low, 2)
                    columns = slice(128 * b, 128 * b + 128)
                    target[row, :, columns] = turned[:, 128 * low : 128 * low + 128]
                by_block[span, b, rows] = out.astype(BF16).reshape(8, 32, HEAD_DIM)


def attention(place, parts):
    quarters = jax.ShapeDtypeStruct((4, HEAD_DIM, 256), BF16)
    return pl.pallas_call(
        attention_kernel,
        out_shape=(quarters, quarters, jax.ShapeDtypeStruct((16, 2, 64, HEAD_DIM), BF16)),
        in_specs=[
            pl.BlockSpec(memory_space=pltpu.SMEM),
            pl.BlockSpec(memory_space=pltpu.VMEM),
        ],
        out_specs=[pl.BlockSpec(memory_space=pltpu.VMEM)] * 3,
        compiler_params=pltpu.CompilerParams(vmem_limit_bytes=40 * MIB),
        cost_estimate=pl.CostEstimate(
            flops=1100000000, bytes_accessed=3 * MIB, transcendentals=2 * MIB
        ),
        name="attention",
    )(place, parts)


def row_sums(place, cotangents, blocks, left, right, sems):
    count = len(blocks) // 2
    x = place[count]
    own, back, ahead, low, high = cotangents

    def copy(j, source, at, distance):
        return pltpu.make_async_copy(
            source.at[pl.ds(at, 2)],
            right.at[2 * j : 2 * j + 2, lax.rem(x - distance + 4, 4)],
            sems.at[j, 2 + distance],
        )

    def copies(j):
        columns = pl.ds(256 * j, 256)
        for half in range(2):
            yield pltpu.make_async_copy(
                blocks[2 * j + half], left.at[4 * half : 4 * half + 4, :, columns], sems.at[j, half]
            )
        for distance, source in ((0, own), (1, back), (3, ahead)):
            yield copy(j, source, place[j], distance)

    for j in range(count):
        for each in copies(j):
            each.start()

        @pl.when(place[j] < 8)
        def _():
            copy(j, low, place[j], 2).start()

        @pl.when(place[j] >= 8)
        def _():
            copy(j, high, place[j] - 8, 2).start()

    for j in range(count):
        for each in copies(j):
            each.wait()
        copy(j, low, 0, 2).wait()
    return jnp.dot(
        left[...].reshape(1024, 256 * count),
        right[...].reshape(256 * count, 768),
        preferred_element_type=F32,
    )


def early_kernel(place, *refs):
    blocks, (out, left, right, sems) = refs[5:-4], refs[-4:]
    out[...] = row_sums(place, refs[:5], blocks, left, right, sems)


def late_kernel(place, *refs):
    blocks, (sent, kept, left, right, sems) = refs[6:-5], refs[-5:]
    total = refs[5][...] + row_sums(place, refs[:5], blocks, left, right, sems)
    for i in range(4):
        kept[i] = total[256 * i : 256 * i + 128]
        sent[i] = total[256 * i + 128 : 256 * i + 256].astype(BF16)


def grad_call(kernel, name, out_shape, place, cotangents, before, blocks):
    vmem = pl.BlockSpec(memory_space=pltpu.VMEM)
    anywhere = pl.BlockSpec(memory_space=pl.ANY)
    count = len(blocks) // 2
    return pl.pallas_call(
        kernel,
        out_shape=out_shape,
        in_specs=[pl.BlockSpec(memory_space=pltpu.SMEM)]
        + [anywhere] * 5
        + [vmem] * len(before)
        + [anywhere] * len(blocks),
        out_specs=jax.tree.map(lambda _: vmem, out_shape),
        scratch_shapes=[
            pltpu.VMEM((8, 128, 256 * count), BF16),
            pltpu.VMEM((2 * count, 4, 32, 768), BF16),
            pltpu.SemaphoreType.DMA((count, 6)),
        ],
        compiler_params=pltpu.CompilerParams(vmem_limit_bytes=58 * MIB),
        cost_estimate=pl.CostEstimate(
            flops=400000000 * count, bytes_accessed=2 * MIB * count, transcendentals=0
        ),
        name=name,
    )(place, *cotangents, *before, *blocks)


def project_kernel(place, *refs):
    nears, fars, weight = refs[:4], refs[4:9], refs[9]
    others, mine, left, sems = refs[10:]

    def copies(d, swapped):
        at = 128 * place[4 + d]
        yield pltpu.make_async_copy(
            nears[d], left.at[swapped, pl.ds(pl.multiple_of(at, 128), 128)], sems.at[d, 0]
        )
        for half, source in enumerate(fars[:2] if d == 0 else fars[d + 1 : d + 2]):
            size = source.shape[0]
            rows = pl.ds(pl.multiple_of(at + size * half, size), size)
            yield pltpu.make_async_copy(source, left.at[1 - swapped, rows], sems.at[d, 1 + half])

    for d in range(4):
        for copy in copies(d, place[d]):
            copy.start()
    for d in range(4):
        for copy in copies(d, place[d]):
            copy.wait()
    rows = left[...].reshape(1024, 2048)
    product = jnp.dot(rows, weight[...], preferred_element_type=F32)
    others[...] = product[:512].astype(BF16)
    mine[...] = product[512:]


def project(place, nears, fars, weight):
    vmem = pl.BlockSpec(memory_space=pltpu.VMEM)
    return pl.pallas_call(
        project_kernel,
        out_shape=(
            jax.ShapeDtypeStruct((512, 768), BF16),
            jax.ShapeDtypeStruct((512, 768), F32),
        ),
        in_specs=[pl.BlockSpec(memory_space=pltpu.SMEM)]
        + [pl.BlockSpec(memory_space=pl.ANY)] * 9
        + [vmem],
        out_specs=(vmem, vmem),
        scratch_shapes=[pltpu.VMEM((2, 512, 2048), BF16), pltpu.SemaphoreType.DMA((4, 3))],
        compiler_params=pltpu.CompilerParams(vmem_limit_bytes=58 * MIB),
        cost_estimate=pl.CostEstimate(
            flops=3200000000, bytes_accessed=10 * MIB, transcendentals=0
        ),
        name="project",
    )(place, *nears, *fars, weight)


def assemble_kernel(distances, place, *refs):
    out = refs[-1]
    y, x = place[0], place[1]
    dy = lax.rem(y - pl.program_id(0) + 4, 4)
    for column in range(4):
        dx = lax.rem(x - column + 4, 4)
        for half in range(2):
            ringed, direct = (dy, dx) if half == 0 else (dx, dy)
            for i, distance in enumerate(distances):

                @pl.when(ringed == distance)
                def _():
                    piece = refs[len(distances) * half + i][direct]
                    out[column, half] = piece.astype(F32)


def assemble(place, pieces):
    vmem = pl.BlockSpec(memory_space=pltpu.VMEM)
    return pl.pallas_call(
        functools.partial(assemble_kernel, (0, 1, 3)),
        grid=(4,),
        out_shape=jax.ShapeDtypeStruct((16, 2, 64, 768), F32),
        in_specs=[pl.BlockSpec(memory_space=pltpu.SMEM)] + [vmem] * 6,
        out_specs=pl.BlockSpec((4, 2, 64, 768), lambda i: (i, 0, 0, 0)),
        compiler_params=pltpu.CompilerParams(vmem_limit_bytes=58 * MIB),
        cost_estimate=pl.CostEstimate(
            flops=2 * MIB, bytes_accessed=9 * MIB, transcendentals=0
        ),
        name="assemble",
    )(place, *pieces)


def finish_kernel(place, top, bottom, _, out, wide, sems):
    y, x = place[0], place[1]
    copies = []
    for d in range(4):
        wide[0, d] = top[d].astype(F32)
        wide[1, d] = bottom[d].astype(F32)
        far_row = 4 * lax.rem(y + 2, 4) + lax.rem(x - d + 4, 4)
        far_column = 4 * lax.rem(y - d + 4, 4) + lax.rem(x + 2, 4)
        for half, at in ((0, far_row), (1, far_column)):
            copy = pltpu.make_async_copy(wide.at[half, d], out.at[at, half], sems.at[half, d])
            copy.start()
            copies.append(copy)
    for copy in copies:
        copy.wait()


def finish(place, top, bottom, begun):
    vmem, anywhere = pl.BlockSpec(memory_space=pltpu.VMEM), pl.BlockSpec(memory_space=pl.ANY)
    return pl.pallas_call(
        finish_kernel,
        out_shape=jax.ShapeDtypeStruct((16, 2, 64, 768), F32),
        in_specs=[pl.BlockSpec(memory_space=pltpu.SMEM), vmem, vmem, anywhere],
        out_specs=anywhere,
        scratch_shapes=[pltpu.VMEM((2, 4, 64, 768), F32), pltpu.SemaphoreType.DMA((2, 4))],
        input_output_aliases={3: 0},
        compiler_params=pltpu.CompilerParams(vmem_limit_bytes=58 * MIB),
        cost_estimate=pl.CostEstimate(
            flops=MIB, bytes_accessed=3 * MIB, transcendentals=0
        ),
        name="finish",
    )(place, top, bottom, begun)


def by_distance(value, axis):
    return jnp.stack([value] + [shift_plane(value, axis, d) for d in (1, 2, 3)])


def around(value, axis, way):
    back, ahead = shift_plane(value, axis, 1), shift_plane(value, axis, -1)
    return [value, back, shift_plane(back if way > 0 else ahead, axis, way), ahead]


def swap_cores(value):
    return lax.ppermute(value, "row", [(0, 1), (1, 0)])


def swap_rows(value, mask):
    return lax.ppermute(value, Y, [(i, i ^ mask) for i in range(4)])


def per_device(projected, out_weight, cotangent):
    yh, yl, x = (lax.axis_index(a) for a in SEQ)
    y = 2 * yh + yl
    core, z = lax.axis_index("row"), lax.axis_index("col")

    by_head = projected.reshape(3, 2, 64, 16, HEAD_DIM).transpose(3, 0, 1, 2, 4)
    parts = lax.all_to_all(by_head, SEQ, 0, 0, tiled=True)

    given = swap_cores(lax.dynamic_slice_in_dim(cotangent, 32 * (1 - core), 32, 1))
    own = lax.dynamic_slice_in_dim(cotangent, 32 * core, 32, 1)
    own, parts = tied(jnp.concatenate([own, given]), parts)

    keep, chip, by_block = attention(jnp.stack([core, yh, yl]), parts)
    chip = swap_cores(chip)
    mine, *others = (jnp.stack([keep[e], chip[e]]) for e in range(4))
    heads = [mine] + [swap_rows(v, e + 1) for e, v in enumerate(others)]
    block, other = jnp.concatenate(heads[:2]), jnp.concatenate(heads[2:])
    back, ahead = shift_plane(own, "x", 1), shift_plane(own, "x", -1)
    low, high = shift_plane(back[:8], "x", 1), shift_plane(ahead[8:], "x", -1)

    first, second, order = [(block, block)], [(other, other)], [z]
    for d in (1, 2, 3):
        if d > 1:
            *first[-1:], second[-2] = pairwise_tied(first[-1], second[-2])
        first.append((shift_z(first[-1][0], 1), shift_z(first[-1][1], -1)))
        second.append((shift_z(second[-1][0], 1), shift_z(second[-1][1], -1)))
        order += [(z - d) % 8, (z + d) % 8]
        if d == 1:
            *first[1:], by_block = tied(first[1], by_block)
            heads = lax.all_to_all(by_block, SEQ, 0, 0, tiled=True)
            tokens = heads.transpose(1, 2, 0, 3).reshape(128, 2048)
        if d == 2:
            *first[2:], low, high = tied(first[2], low, high)
    first[3], second[3] = pairwise_tied(first[3], second[3])
    cotangents = [own, back, ahead, low, high]
    last = shift_z(first[3][0], 1), shift_z(second[3][1], -1)
    *last, tokens = tied(*last, tokens)
    blocks = [first[0][0], second[0][0]]
    for one, two in zip(first[1:], second[1:]):
        blocks += [one[0], two[0], one[1], two[1]]
    blocks += last
    order = (2 * jnp.stack(order + [(z + 4) % 8]) + 8 * core) % 16
    spot = x.reshape(1)
    rows = jax.ShapeDtypeStruct((1024, 768), F32)
    early = grad_call(
        early_kernel,
        "early",
        rows,
        jnp.concatenate([order[:5], spot]),
        cotangents,
        [],
        blocks[:10],
    )
    sent, kept = grad_call(
        late_kernel,
        "late",
        (
            jax.ShapeDtypeStruct((4, 128, 768), BF16),
            jax.ShapeDtypeStruct((4, 128, 768), F32),
        ),
        jnp.concatenate([order[5:], spot]),
        cotangents,
        [early],
        blocks[10:],
    )
    kept = kept + swap_cores(sent).astype(F32)
    rows = kept[0]
    for e in (1, 2, 3):
        rows = rows + swap_rows(kept[e].astype(BF16), e).astype(F32)
    rows = rows.astype(BF16)

    ups, downs = [tokens, shift_z(tokens, 1)], [tokens, shift_z(tokens, -1)]
    ups[1], downs[1], rows = tied(ups[1], downs[1], rows)
    ups.append(shift_z(ups[1], 1))
    downs.append(shift_z(downs[1], -1))
    top, bottom = by_distance(rows[:64], "x"), by_distance(rows[64:], Y)
    ups[2], downs[2], top, bottom = tied(ups[2], downs[2], top, bottom)
    ups.append(shift_z(ups[2], 1))
    downs.append(shift_z(downs[2], -1))
    top, bottom = around(top, Y, 1), around(bottom, "x", -1)
    ups[3], downs[3], top[1], top[3], bottom[1], bottom[3] = tied(
        ups[3], downs[3], top[1], top[3], bottom[1], bottom[3]
    )
    last = [shift_z(ups[3][:64], 1), shift_z(downs[3][64:], -1)]
    place = jnp.stack([y, x])
    begun = assemble(place, top[:2] + top[3:] + bottom[:2] + bottom[3:])
    *last, top[2], bottom[2], begun = tied(*last, top[2], bottom[2], begun)
    here = [((z - d) % 8 // 4 == core).astype(jnp.int32) for d in range(4)]
    slots = [(z - d) % 4 for d in range(4)]
    sent, mine = project(
        jnp.stack(here + slots), ups, last + [downs[3], downs[2], downs[1]], out_weight
    )
    sent = swap_cores(sent)
    weight_grad = finish(place, top[2], bottom[2], begun).reshape(2048, 768)
    mixed = (mine + sent.astype(F32)).astype(BF16).reshape(8, 64, 768)
    return mixed, weight_grad


def solution(mesh):
    fine = Mesh(mesh.devices.reshape(2, 2, 4, 2, 8), SEQ + ("row", "col"))
    return jax.shard_map(
        per_device,
        mesh=fine,
        in_specs=(P(None, "col", SEQ, "row"), P("row", "col"), P("row", SEQ, "col")),
        out_specs=(P("row", SEQ, "col"), P("row", "col")),
        check_vma=False,
    )
```

```python
import functools
import math

import jax
import jax.numpy as jnp
from jax import lax
from jax.experimental import pallas as pl
from jax.experimental.pallas import tpu as pltpu
from jax.sharding import Mesh, PartitionSpec as P

HEAD_DIM = 128
F32 = jnp.float32
BF16 = jnp.bfloat16
Y = ("yh", "yl")
SEQ = ("yh", "yl", "x")
MIB = 1024 * 1024


def ring(size, shift):
    return [(i, (i + shift) % size) for i in range(size)]


def tied(*values):
    return lax.optimization_barrier(values)


def pairwise_tied(one, two):
    values = tied(*one, *two)
    return tuple(values[:2]), tuple(values[2:])


def shift_z(value, step):
    return lax.ppermute(value, "col", ring(8, step))


def shift_plane(value, axis, step):
    return lax.ppermute(value, axis, ring(4, step))


def attention_kernel(place, parts, keep, chip, by_block):
    core, upper, lower = place[0], place[1], place[2]
    scale = math.log2(math.e) / math.sqrt(HEAD_DIM)
    for b in range(2):
        keys = parts[:, 1, b].reshape(1024, HEAD_DIM)
        values = parts[:, 2, b].reshape(1024, HEAD_DIM)
        for far in range(2):
            rows = pl.ds(pl.multiple_of(32 * lax.rem(core + far, 2), 32), 32)
            target = chip if far else keep
            for away in range(2):
                span = pl.ds(8 * lax.rem(upper + away, 2), 8)
                queries = parts[span, 0, b, rows].reshape(256, HEAD_DIM)
                scores = lax.dot_general(
                    queries, keys, (((1,), (1,)), ((), ())), preferred_element_type=F32
                )
                top = jnp.max(scores, axis=1, keepdims=True)
                exps = jnp.exp2((scores - top) * scale)
                total = jnp.sum(exps, axis=1, keepdims=True)
                out = jnp.dot(exps.astype(BF16), values, preferred_element_type=F32) / total
                turned = out.T.astype(BF16)
                for low in range(2):
                    row = 2 * away + lax.rem(lower + low, 2)
                    columns = slice(128 * b, 128 * b + 128)
                    target[row, :, columns] = turned[:, 128 * low : 128 * low + 128]
                by_block[span, b, rows] = out.astype(BF16).reshape(8, 32, HEAD_DIM)


def attention(place, parts):
    quarters = jax.ShapeDtypeStruct((4, HEAD_DIM, 256), BF16)
    return pl.pallas_call(
        attention_kernel,
        out_shape=(quarters, quarters, jax.ShapeDtypeStruct((16, 2, 64, HEAD_DIM), BF16)),
        in_specs=[
            pl.BlockSpec(memory_space=pltpu.SMEM),
            pl.BlockSpec(memory_space=pltpu.VMEM),
        ],
        out_specs=[pl.BlockSpec(memory_space=pltpu.VMEM)] * 3,
        compiler_params=pltpu.CompilerParams(vmem_limit_bytes=40 * MIB),
        cost_estimate=pl.CostEstimate(
            flops=1100000000, bytes_accessed=3 * MIB, transcendentals=2 * MIB
        ),
        name="attention",
    )(place, parts)


def row_sums(place, cotangents, blocks, left, right, sems):
    count = len(blocks) // 2
    x = place[count]
    own, back, ahead, low, high = cotangents

    def copy(j, source, at, distance):
        return pltpu.make_async_copy(
            source.at[pl.ds(at, 2)],
            right.at[2 * j : 2 * j + 2, lax.rem(x - distance + 4, 4)],
            sems.at[j, 2 + distance],
        )

    def copies(j):
        columns = pl.ds(256 * j, 256)
        for half in range(2):
            yield pltpu.make_async_copy(
                blocks[2 * j + half], left.at[4 * half : 4 * half + 4, :, columns], sems.at[j, half]
            )
        for distance, source in ((0, own), (1, back), (3, ahead)):
            yield copy(j, source, place[j], distance)

    for j in range(count):
        for each in copies(j):
            each.start()

        @pl.when(place[j] < 8)
        def _():
            copy(j, low, place[j], 2).start()

        @pl.when(place[j] >= 8)
        def _():
            copy(j, high, place[j] - 8, 2).start()

    for j in range(count):
        for each in copies(j):
            each.wait()
        copy(j, low, 0, 2).wait()
    return jnp.dot(
        left[...].reshape(1024, 256 * count),
        right[...].reshape(256 * count, 768),
        preferred_element_type=F32,
    )


def early_kernel(place, *refs):
    blocks, (out, left, right, sems) = refs[5:-4], refs[-4:]
    out[...] = row_sums(place, refs[:5], blocks, left, right, sems)


def late_kernel(place, *refs):
    blocks, (sent, kept, left, right, sems) = refs[6:-5], refs[-5:]
    total = refs[5][...] + row_sums(place, refs[:5], blocks, left, right, sems)
    for i in range(4):
        kept[i] = total[256 * i : 256 * i + 128]
        sent[i] = total[256 * i + 128 : 256 * i + 256].astype(BF16)


def grad_call(kernel, name, out_shape, place, cotangents, before, blocks):
    vmem = pl.BlockSpec(memory_space=pltpu.VMEM)
    anywhere = pl.BlockSpec(memory_space=pl.ANY)
    count = len(blocks) // 2
    return pl.pallas_call(
        kernel,
        out_shape=out_shape,
        in_specs=[pl.BlockSpec(memory_space=pltpu.SMEM)]
        + [anywhere] * 5
        + [vmem] * len(before)
        + [anywhere] * len(blocks),
        out_specs=jax.tree.map(lambda _: vmem, out_shape),
        scratch_shapes=[
            pltpu.VMEM((8, 128, 256 * count), BF16),
            pltpu.VMEM((2 * count, 4, 32, 768), BF16),
            pltpu.SemaphoreType.DMA((count, 6)),
        ],
        compiler_params=pltpu.CompilerParams(vmem_limit_bytes=58 * MIB),
        cost_estimate=pl.CostEstimate(
            flops=400000000 * count, bytes_accessed=2 * MIB * count, transcendentals=0
        ),
        name=name,
    )(place, *cotangents, *before, *blocks)


def products(blocks, weight, left, sems):
    copies, at = [], 0
    for j, block in enumerate(blocks):
        size = block.shape[0]
        copies.append(pltpu.make_async_copy(block, left.at[at : at + size], sems.at[j]))
        copies[-1].start()
        at += size
    for copy in copies:
        copy.wait()
    return jnp.dot(left[...], weight[...], preferred_element_type=F32)


def project_kernel(weight, *refs):
    blocks, (out, left, sems) = refs[:-3], refs[-3:]
    out[...] = products(blocks, weight, left, sems)


def place_kernel(place, ready, weight, *refs):
    blocks, (others, mine, left, sems) = refs[:-4], refs[-4:]
    late = products(blocks, weight, left, sems)
    for j in range(8):
        block = ready[128 * j : 128 * j + 128] if j < 5 else late[128 * j - 640 : 128 * j - 512]
        rows = pl.ds(pl.multiple_of(128 * place[8 + j], 128), 128)

        @pl.when(place[j] == 1)
        def _():
            mine[rows] = block

        @pl.when(place[j] == 0)
        def _():
            others[rows] = block.astype(BF16)


def project_call(kernel, name, out_shape, arrays, blocks, rows):
    vmem, anywhere = pl.BlockSpec(memory_space=pltpu.VMEM), pl.BlockSpec(memory_space=pl.ANY)
    smem = [pl.BlockSpec(memory_space=pltpu.SMEM)] if len(arrays) > 1 else []
    return pl.pallas_call(
        kernel,
        out_shape=out_shape,
        in_specs=smem + [vmem] * (len(arrays) - len(smem)) + [anywhere] * len(blocks),
        out_specs=jax.tree.map(lambda _: vmem, out_shape),
        scratch_shapes=[pltpu.VMEM((rows, 2048), BF16), pltpu.SemaphoreType.DMA((len(blocks),))],
        compiler_params=pltpu.CompilerParams(vmem_limit_bytes=58 * MIB),
        cost_estimate=pl.CostEstimate(
            flops=3200000 * rows, bytes_accessed=10240 * rows, transcendentals=0
        ),
        name=name,
    )(*arrays, *blocks)


def assemble_kernel(distances, place, *refs):
    out = refs[-1]
    y, x = place[0], place[1]
    dy = lax.rem(y - pl.program_id(0) + 4, 4)
    for column in range(4):
        dx = lax.rem(x - column + 4, 4)
        for half in range(2):
            ringed, direct = (dy, dx) if half == 0 else (dx, dy)
            for i, distance in enumerate(distances):

                @pl.when(ringed == distance)
                def _():
                    piece = refs[len(distances) * half + i][direct]
                    out[column, half] = piece.astype(F32)


def assemble(place, pieces):
    vmem = pl.BlockSpec(memory_space=pltpu.VMEM)
    return pl.pallas_call(
        functools.partial(assemble_kernel, (0, 1, 3)),
        grid=(4,),
        out_shape=jax.ShapeDtypeStruct((16, 2, 64, 768), F32),
        in_specs=[pl.BlockSpec(memory_space=pltpu.SMEM)] + [vmem] * 6,
        out_specs=pl.BlockSpec((4, 2, 64, 768), lambda i: (i, 0, 0, 0)),
        compiler_params=pltpu.CompilerParams(vmem_limit_bytes=58 * MIB),
        cost_estimate=pl.CostEstimate(
            flops=2 * MIB, bytes_accessed=9 * MIB, transcendentals=0
        ),
        name="assemble",
    )(place, *pieces)


def finish_kernel(place, top, bottom, _, out, wide, sems):
    y, x = place[0], place[1]
    copies = []
    for d in range(4):
        wide[0, d] = top[d].astype(F32)
        wide[1, d] = bottom[d].astype(F32)
        far_row = 4 * lax.rem(y + 2, 4) + lax.rem(x - d + 4, 4)
        far_column = 4 * lax.rem(y - d + 4, 4) + lax.rem(x + 2, 4)
        for half, at in ((0, far_row), (1, far_column)):
            copy = pltpu.make_async_copy(wide.at[half, d], out.at[at, half], sems.at[half, d])
            copy.start()
            copies.append(copy)
    for copy in copies:
        copy.wait()


def finish(place, top, bottom, begun):
    vmem, anywhere = pl.BlockSpec(memory_space=pltpu.VMEM), pl.BlockSpec(memory_space=pl.ANY)
    return pl.pallas_call(
        finish_kernel,
        out_shape=jax.ShapeDtypeStruct((16, 2, 64, 768), F32),
        in_specs=[pl.BlockSpec(memory_space=pltpu.SMEM), vmem, vmem, anywhere],
        out_specs=anywhere,
        scratch_shapes=[pltpu.VMEM((2, 4, 64, 768), F32), pltpu.SemaphoreType.DMA((2, 4))],
        input_output_aliases={3: 0},
        compiler_params=pltpu.CompilerParams(vmem_limit_bytes=58 * MIB),
        cost_estimate=pl.CostEstimate(
            flops=MIB, bytes_accessed=3 * MIB, transcendentals=0
        ),
        name="finish",
    )(place, top, bottom, begun)


def by_distance(value, axis):
    return jnp.stack([value] + [shift_plane(value, axis, d) for d in (1, 2, 3)])


def around(value, axis, way):
    back, ahead = shift_plane(value, axis, 1), shift_plane(value, axis, -1)
    return [value, back, shift_plane(back if way > 0 else ahead, axis, way), ahead]


def swap_cores(value):
    return lax.ppermute(value, "row", [(0, 1), (1, 0)])


def swap_rows(value, mask):
    return lax.ppermute(value, Y, [(i, i ^ mask) for i in range(4)])


def per_device(projected, out_weight, cotangent):
    yh, yl, x = (lax.axis_index(a) for a in SEQ)
    y = 2 * yh + yl
    core, z = lax.axis_index("row"), lax.axis_index("col")

    by_head = projected.reshape(3, 2, 64, 16, HEAD_DIM).transpose(3, 0, 1, 2, 4)
    parts = lax.all_to_all(by_head, SEQ, 0, 0, tiled=True)

    given = swap_cores(lax.dynamic_slice_in_dim(cotangent, 32 * (1 - core), 32, 1))
    own = lax.dynamic_slice_in_dim(cotangent, 32 * core, 32, 1)
    own, parts = tied(jnp.concatenate([own, given]), parts)

    keep, chip, by_block = attention(jnp.stack([core, yh, yl]), parts)
    chip = swap_cores(chip)
    mine, *others = (jnp.stack([keep[e], chip[e]]) for e in range(4))
    heads = [mine] + [swap_rows(v, e + 1) for e, v in enumerate(others)]
    block, other = jnp.concatenate(heads[:2]), jnp.concatenate(heads[2:])
    back, ahead = shift_plane(own, "x", 1), shift_plane(own, "x", -1)
    low, high = shift_plane(back[:8], "x", 1), shift_plane(ahead[8:], "x", -1)

    first, second, order = [(block, block)], [(other, other)], [z]
    for d in (1, 2, 3):
        if d > 1:
            *first[-1:], second[-2] = pairwise_tied(first[-1], second[-2])
        first.append((shift_z(first[-1][0], 1), shift_z(first[-1][1], -1)))
        second.append((shift_z(second[-1][0], 1), shift_z(second[-1][1], -1)))
        order += [(z - d) % 8, (z + d) % 8]
        if d == 1:
            *first[1:], by_block = tied(first[1], by_block)
            heads = lax.all_to_all(by_block, SEQ, 0, 0, tiled=True)
            tokens = heads.transpose(1, 2, 0, 3).reshape(128, 2048)
        if d == 2:
            *first[2:], low, high = tied(first[2], low, high)
    first[3], second[3] = pairwise_tied(first[3], second[3])
    cotangents = [own, back, ahead, low, high]
    last = shift_z(first[3][0], 1), shift_z(second[3][1], -1)
    *last, tokens = tied(*last, tokens)
    blocks = [first[0][0], second[0][0]]
    for one, two in zip(first[1:], second[1:]):
        blocks += [one[0], two[0], one[1], two[1]]
    blocks += last
    order = (2 * jnp.stack(order + [(z + 4) % 8]) + 8 * core) % 16
    spot = x.reshape(1)
    rows = jax.ShapeDtypeStruct((1024, 768), F32)
    early = grad_call(
        early_kernel,
        "early",
        rows,
        jnp.concatenate([order[:5], spot]),
        cotangents,
        [],
        blocks[:10],
    )
    sent, kept = grad_call(
        late_kernel,
        "late",
        (
            jax.ShapeDtypeStruct((4, 128, 768), BF16),
            jax.ShapeDtypeStruct((4, 128, 768), F32),
        ),
        jnp.concatenate([order[5:], spot]),
        cotangents,
        [early],
        blocks[10:],
    )
    kept = kept + swap_cores(sent).astype(F32)
    rows = kept[0]
    for e in (1, 2, 3):
        rows = rows + swap_rows(kept[e].astype(BF16), e).astype(F32)
    rows = rows.astype(BF16)

    ups, downs = [tokens, shift_z(tokens, 1)], [tokens, shift_z(tokens, -1)]
    ups[1], downs[1], rows = tied(ups[1], downs[1], rows)
    ups.append(shift_z(ups[1], 1))
    downs.append(shift_z(downs[1], -1))
    top, bottom = by_distance(rows[:64], "x"), by_distance(rows[64:], Y)
    ups[2], downs[2], top, bottom = tied(ups[2], downs[2], top, bottom)
    ups.append(shift_z(ups[2], 1))
    downs.append(shift_z(downs[2], -1))
    top, bottom = around(top, Y, 1), around(bottom, "x", -1)
    ready = project_call(
        project_kernel,
        "project",
        jax.ShapeDtypeStruct((640, 768), F32),
        [out_weight],
        [tokens, ups[1], downs[1], ups[2], downs[2]],
        640,
    )
    ready, ups[3], downs[3], top[1], top[3], bottom[1], bottom[3] = tied(
        ready, ups[3], downs[3], top[1], top[3], bottom[1], bottom[3]
    )
    last = [shift_z(ups[3][:64], 1), shift_z(downs[3][64:], -1)]
    place = jnp.stack([y, x])
    begun = assemble(place, top[:2] + top[3:] + bottom[:2] + bottom[3:])
    *last, top[2], bottom[2], begun = tied(*last, top[2], bottom[2], begun)
    planes = [(z + d) % 8 for d in (0, -1, 1, -2, 2, -3, 3, 4)]
    here = [(p // 4 == core).astype(jnp.int32) for p in planes]
    sent, mine = project_call(
        place_kernel,
        "place",
        (
            jax.ShapeDtypeStruct((512, 768), BF16),
            jax.ShapeDtypeStruct((512, 768), F32),
        ),
        [jnp.stack(here + [p % 4 for p in planes]), ready, out_weight],
        [ups[3], downs[3], *last],
        384,
    )
    sent = swap_cores(sent)
    weight_grad = finish(place, top[2], bottom[2], begun).reshape(2048, 768)
    mixed = (mine + sent.astype(F32)).astype(BF16).reshape(8, 64, 768)
    return mixed, weight_grad


def solution(mesh):
    fine = Mesh(mesh.devices.reshape(2, 2, 4, 2, 8), SEQ + ("row", "col"))
    return jax.shard_map(
        per_device,
        mesh=fine,
        in_specs=(P(None, "col", SEQ, "row"), P("row", "col"), P("row", SEQ, "col")),
        out_specs=(P("row", SEQ, "col"), P("row", "col")),
        check_vma=False,
    )
```
